256 devices in a mesh: dp: 32 (over y, x, core), mp: 8 (over z).
Axes of the slice: x: 4, y: 4, z: 8, core: 2. Of those that a mesh axis runs over, the one named last changes fastest.
Arguments:
- hidden: bfloat16 [768, 256, 4096], P(('dp', 'mp')), may hold values from -6 to 6
- lengths: int32 [768], P(('dp', 'mp')), may hold values from 32 to 256, as said below
- list_ids: int32 [768], P('dp'), may hold values from 0 to 65535, as said below
- gain: bfloat16 [4096], replicated, may hold values from 0.099609375 to 1.8984375
- head: bfloat16 [4096, 1024], P('dp', 'mp'), may hold values from -0.09375 to 0.09375
- list_slot: int32 [65536], replicated, may hold values from 0 to 65535, as said below
- centroids: bfloat16 [65536, 1024], P('dp'), may hold values from -0.59765625 to 0.59765625
- rotation: bfloat16 [1024, 1024], P('mp'), may hold values from -0.1875 to 0.1875
Outputs:
- codes: bfloat16 [768, 1024], P('dp', 'mp')
- scales: bfloat16 [768, 16], P('dp', 'mp')
The draws below stay inside these ranges and needn't reach their ends.
Inputs may be any that keep to these rules, and one draw needn't show every extreme that they name: `list_ids`: in each aligned block of 24 passages, at most 2 have lists in one range of 2048 lists (list id // 2048); one range holds exactly 2 of them in every block. Each list's row in the centroid table; list_slot[l] // 2048 equals l // 2048, and each row of a range once. `lengths`: some passage has exactly 256 valid tokens.
All inputs are finite; a program needn't handle non-finite values. Where the reference program divides by a largest or mean magnitude, that divisor is 1e-20 or more.
Results may differ from the reference program's by a relative error of at most 0.013.
Values may be sent and summed in bfloat16 or wider, within the bound.
A program may use at most 64 MiB of HBM per device.

```python
import jax
import jax.numpy as jnp
from jax import lax

D = 4096
EMB = 1024
BLOCK = 64
LISTS = 65536
LEN = 256
PASS_DEV = 24
PASSAGES = 768
LISTS_OWN = 2048
CAP = 2


def draw_lengths(key, part):
    values = jax.random.randint(key, (PASSAGES,), LEN // 8, LEN + 1)
    return values.at[0].set(LEN).astype(jnp.int32)


def draw_list_slot(key, part):
    ranges = LISTS // LISTS_OWN
    keys = jax.random.split(key, ranges)
    perms = jax.vmap(lambda k: jax.random.permutation(k, LISTS_OWN))(keys)
    offsets = jnp.arange(ranges, dtype=jnp.int32)[:, None] * LISTS_OWN
    return (perms.astype(jnp.int32) + offsets).reshape(-1).astype(jnp.int32)


def draw_list_ids(key, part):
    ranges = LISTS // LISTS_OWN
    total_slots = ranges * CAP
    busiest = jax.random.randint(jax.random.fold_in(key, 7), (), 0, ranges)
    blocks = PASSAGES // PASS_DEV

    def one_block(block_key):
        first_key, second_key = jax.random.split(block_key)
        shuffled = jax.random.permutation(first_key, total_slots).astype(jnp.int32)
        places = jnp.arange(total_slots, dtype=jnp.int32)
        score = jnp.where(places // CAP == busiest, places - total_slots, shuffled)
        order = jnp.argsort(score, stable=True).astype(jnp.int32)
        chosen = order[:PASS_DEV] // CAP
        mixing = jax.random.permutation(second_key, PASS_DEV)
        return chosen[mixing]
    owners = jax.vmap(one_block)(jax.random.split(jax.random.fold_in(key, 1), blocks)).reshape(-1)
    within = jax.random.randint(jax.random.fold_in(key, 2), (PASSAGES,), 0, LISTS_OWN)
    return (owners * LISTS_OWN + within).astype(jnp.int32)


def level_of(rng, extent, pieces, low, top_value):
    def one(axis_at, blocks):
        draws = jax.random.uniform(jax.random.fold_in(jax.random.fold_in(rng, 6), axis_at), (blocks,), jnp.float32, low / len(pieces), top_value / len(pieces))
        return jnp.repeat(jnp.exp(draws), extent[axis_at] // blocks).reshape((-1,) + (1,) * (len(extent) - axis_at - 1))

    loudness = one(*pieces[0])
    for cut in pieces[1:]:
        loudness = loudness * one(*cut)
    return loudness


def gaussian(key, dims, width, bound, shards=(), kind=jnp.bfloat16):
    values = jax.random.normal(key, dims, jnp.float32) * width
    if len(shards) > 0:
        values = level_of(key, dims, shards, -0.22, 0.18) * values
    return jnp.clip(values, min=-bound, max=bound).astype(kind)


def setup_inputs(seed: int = 0) -> dict:
    key_of = jax.random.split(jax.random.key(seed), 9)
    hidden = gaussian(key_of[0], (PASSAGES, LEN, D), 1.0, 6.0, ((0, 256),))
    lengths = draw_lengths(jax.random.fold_in(key_of[8], 71), 0)
    list_ids = draw_list_ids(jax.random.fold_in(key_of[8], 71), 0)
    gain = jnp.clip(1.0 + 0.18 * jax.random.normal(key_of[3], (D,), jnp.float32), 0.099609375, 1.8984375).astype(jnp.bfloat16)
    head = gaussian(key_of[4], (D, EMB), D ** -0.5, 0.09375, ((0, 32), (1, 8)))
    list_slot = draw_list_slot(jax.random.fold_in(key_of[8], 71), 0)
    centroids = gaussian(key_of[6], (LISTS, EMB), 0.1, 0.59765625, ((0, 32),))
    rotation = gaussian(key_of[7], (EMB, EMB), EMB ** -0.5, 0.1875, ((0, 8),))
    return {"hidden": hidden, "lengths": lengths, "list_ids": list_ids, "gain": gain, "head": head, "list_slot": list_slot, "centroids": centroids, "rotation": rotation}


def encode(rows, cents, rotation):
    resid = (rows.astype(jnp.float32) - cents.astype(jnp.float32)).astype(jnp.bfloat16)
    rotated = jnp.dot(resid, rotation, preferred_element_type=jnp.float32)
    blocks = rotated.reshape(rotated.shape[0], EMB // BLOCK, BLOCK)
    scale = lax.optimization_barrier(jnp.max(jnp.abs(blocks), axis=-1)) + 1e-06
    codes = (blocks / scale[:, :, None]).reshape(rotated.shape).astype(jnp.bfloat16)
    return (codes, scale.astype(jnp.bfloat16))

def reference(hidden, lengths, list_ids, gain, head, list_slot, centroids, rotation):
    gain_f = gain.astype(jnp.float32)

    def pool_one(pair):
        states, length = pair
        states = states.astype(jnp.float32)
        mean_square = lax.optimization_barrier(jnp.mean(states * states, axis=-1, keepdims=True))
        normed = states * lax.rsqrt(mean_square + 1e-05) * gain_f
        valid = jnp.arange(LEN, dtype=jnp.int32) < length
        total = lax.optimization_barrier(jnp.sum(jnp.where(valid[:, None], normed, 0.0), axis=0))
        return total / length.astype(jnp.float32)
    pooled = lax.map(pool_one, (hidden, lengths)).astype(jnp.bfloat16)
    projected = jnp.dot(pooled, head, preferred_element_type=jnp.float32).astype(jnp.bfloat16)
    slot = list_slot[list_ids].astype(jnp.int32)
    cents = centroids[slot]
    codes, scales = encode(projected, cents, rotation)
    return (codes, scales)
```

```python
import jax
import jax.numpy as jnp
from jax import lax
from jax.experimental import pallas as pl
from jax.experimental.pallas import tpu as pltpu
from jax.sharding import PartitionSpec as P

MESH = pl.DeviceIdType.MESH
F32 = jnp.float32
BF16 = jnp.bfloat16
EPS = 1e-05
HALF = 128
NT = (((1,), (1,)), ((), ()))


def iota(shape, axis):
    return lax.broadcasted_iota(jnp.int32, shape, axis)


def kernel(
    hidden, lengths, list_ids, gain, head, list_slot, centroids, rotation,
    codes_ref, scales_ref,
    hid_v, len_v, ids_all, gain_v, hbuf, slot_v, cent_v, rot_v,
    row_send, row_recv, pool_t, pbuf, pool_f, part_send, part_recv,
    sem_loc, sem_hid, s_ids, r_ids, s_row, r_row, s_pool, r_pool,
    s_h1, r_h1, s_h2, r_h2, s_sib, r_sib, s_part, r_part,
):
    g = lax.axis_index("dp")
    m = lax.axis_index("mp")
    core = lax.rem(g, 2)
    x = lax.rem(g // 2, 4)
    y = g // 8
    first = jnp.where(core == 0, x, y)
    second = jnp.where(core == 0, y, x)
    f_mul = 2 + 6 * core
    s_mul = 8 - 6 * core
    sibling = g + 1 - 2 * core

    def local(src, dst, i):
        return pltpu.make_async_copy(src, dst, sem_loc.at[i])

    loads = [
        local(head, hbuf.at[core, second, first], 0),
        local(list_ids, ids_all.at[g], 1),
        local(lengths, len_v, 2),
        local(gain, gain_v, 3),
        local(list_slot.at[g], slot_v, 4),
        local(centroids.at[:, pl.ds(pl.multiple_of(m * 128, 128), 128)], cent_v, 5),
        local(rotation, rot_v, 6),
    ]
    chunks = []
    for p in range(3):
        for h in range(2):
            rows = pl.ds(h * HALF, HALF)
            chunks.append(
                pltpu.make_async_copy(
                    hidden.at[p, rows], hid_v.at[p, rows], sem_hid.at[2 * p + h]
                )
            )
    for c in loads[:4]:
        c.start()
    for c in chunks[:2]:
        c.start()
    for c in loads[4:6]:
        c.start()
    for c in chunks[2:]:
        c.start()
    loads[6].start()

    barrier = pltpu.get_barrier_semaphore()

    def greet_plane(i, carry):
        pl.semaphore_signal(
            barrier, inc=1, device_id=(lax.rem(g + 1 + i, 32), m), device_id_type=MESH
        )
        return carry

    def greet_z(i, carry):
        pl.semaphore_signal(
            barrier, inc=1, device_id=(g, lax.rem(m + 1 + i, 8)), device_id_type=MESH
        )
        return carry

    lax.fori_loop(0, 31, greet_plane, 0)
    lax.fori_loop(0, 7, greet_z, 0)
    loads[0].wait()
    loads[1].wait()
    pl.semaphore_wait(barrier, 38)

    own = hbuf.at[core, second, first]
    for d in range(1, 4):
        f2 = lax.rem(first + d, 4)
        pltpu.make_async_remote_copy(
            own, own, s_h1, r_h1, device_id=(f2 * f_mul + second * s_mul + core, m), device_id_type=MESH
        ).start()

    def send_ids(i, carry):
        pltpu.make_async_remote_copy(
            ids_all.at[g], ids_all.at[g], s_ids, r_ids,
            device_id=(lax.rem(g + 1 + i, 32), m), device_id_type=MESH,
        ).start()
        return carry

    lax.fori_loop(0, 31, send_ids, 0)
    loads[2].wait()
    loads[3].wait()
    gain_f = gain_v[...].astype(F32)
    ones = jnp.ones((8, 128), BF16)

    def pool(p):
        total = jnp.zeros((8, 4096), F32)
        length = len_v[:, p : p + 1]
        for h in range(2):
            chunks[2 * p + h].wait()
            rows = pl.ds(h * HALF, HALF)
            acc = jnp.zeros((HALF, 128), F32)
            for c in range(32):
                v = hid_v[p, rows, c * 128 : (c + 1) * 128].astype(F32)
                acc += v * v
            hi = acc.astype(BF16)
            lo = (acc - hi.astype(F32)).astype(BF16)
            square = lax.dot_general(ones, hi, NT, preferred_element_type=F32)
            square += lax.dot_general(ones, lo, NT, preferred_element_type=F32)
            token = iota((8, HALF), 1) + h * HALF
            w = jnp.where(token < length, lax.rsqrt(square * (1.0 / 4096) + EPS), 0.0)
            w = w / length.astype(F32)
            w_hi = w.astype(BF16).astype(F32)
            which = iota((8, HALF), 0)
            lhs = jnp.where(which == 0, w_hi, jnp.where(which == 1, w - w_hi, 0.0)).astype(BF16)
            total += jnp.dot(lhs, hid_v[p, rows, :], preferred_element_type=F32)
        line = total[0:1] + total[1:2]
        for c in range(32):
            pool_t[p, c : c + 1, :] = line[:, c * 128 : (c + 1) * 128]
        pbuf[m, p] = (pool_t[p] * gain_f).astype(BF16)
        mine = pbuf.at[m, p]
        for d in range(1, 8):
            pltpu.make_async_remote_copy(
                mine, mine, s_pool.at[p], r_pool.at[p],
                device_id=(g, lax.rem(m + d, 8)), device_id_type=MESH,
            ).start()

    def wait_many(ref, sem):
        pltpu.make_async_copy(ref, ref, sem).wait()

    pool(0)

    wait_many(hbuf.at[core, 0, pl.ds(0, 3)], r_h1)

    def send_second(d):
        s2 = lax.rem(second + d, 4)
        part = hbuf.at[core, second]
        pltpu.make_async_remote_copy(
            part, part, s_h2, r_h2.at[second],
            device_id=(first * f_mul + s2 * s_mul + core, m), device_id_type=MESH,
        ).start()

    for d in (1, 3, 2):
        send_second(d)

    def to_sibling(s):
        part = hbuf.at[core, s]
        pltpu.make_async_remote_copy(
            part, part, s_sib, r_sib.at[s], device_id=(sibling, m), device_id_type=MESH
        ).start()

    to_sibling(second)

    pool(1)

    wait_many(ids_all.at[pl.ds(0, 31)], r_ids)
    loads[4].wait()
    loads[5].wait()
    ids = ids_all[:, 0, :]
    match = (ids >> 11) == g
    lane = iota(ids.shape, 1).astype(F32)
    low = (ids & 2047).astype(F32)
    lo_lane = jnp.min(jnp.where(match, lane, 1e3), axis=1, keepdims=True)
    hi_lane = jnp.max(jnp.where(match, lane, -1.0), axis=1, keepdims=True)
    v0 = jnp.sum(jnp.where(lane == lo_lane, low, 0.0), axis=1, keepdims=True)
    v1 = jnp.sum(jnp.where(lane == hi_lane, low, 0.0), axis=1, keepdims=True)
    wanted = jnp.concatenate([v0, v1], axis=0)
    column = iota((64, 128), 1).astype(F32)
    found = jnp.zeros((64, 128), F32)
    for c in range(16):
        slots = (slot_v[c : c + 1, :] & 2047).astype(F32)
        found += jnp.where(wanted == column + c * 128.0, slots, 0.0)
    found = jnp.sum(found, axis=1, keepdims=True)
    picked = jnp.zeros((64, 128), F32)
    for c in range(16):
        hot = jnp.where(found == column + c * 128.0, 1.0, 0.0).astype(BF16)
        picked += jnp.dot(hot, cent_v[c * 128 : (c + 1) * 128, :], preferred_element_type=F32)
    row_send[:, 0, :] = picked[:32]
    row_send[:, 1, :] = picked[32:]

    def send_rows(i, carry):
        to = lax.rem(g + 1 + i, 32)
        pltpu.make_async_remote_copy(
            row_send.at[to], row_recv.at[g], s_row, r_row, device_id=(to, m), device_id_type=MESH
        ).start()
        return carry

    lax.fori_loop(0, 31, send_rows, 0)
    row_recv[g] = row_send[g]

    pool(2)

    for d in (1, 3, 2):
        s2 = lax.rem(second + d, 4)
        pltpu.make_async_copy(hbuf.at[core, s2], hbuf.at[core, s2], r_h2.at[s2]).wait()
        to_sibling(s2)

    wait_many(row_recv.at[pl.ds(0, 31)], r_row)
    mine = (ids_all[g] >> 11).astype(F32)
    r24 = iota((24, 24), 0)
    c24 = iota((24, 24), 1)
    along = jnp.broadcast_to(mine, (24, 24))
    owner = jnp.sum(jnp.where(r24 == c24, along, 0.0), axis=1, keepdims=True)
    again = jnp.max(jnp.where((along == owner) & (c24 < r24), 1.0, 0.0), axis=1, keepdims=True)
    which = iota((24, 32), 1).astype(F32)
    here = jnp.where(owner == which, 1.0, 0.0)
    cents = jnp.dot(
        (here * (1.0 - again)).astype(BF16), row_recv[:, 0, :].astype(BF16), preferred_element_type=F32
    )
    cents += jnp.dot(
        (here * again).astype(BF16), row_recv[:, 1, :].astype(BF16), preferred_element_type=F32
    )

    for p in range(3):
        wait_many(pbuf.at[pl.ds(0, 7), p], r_pool.at[p])
    pool_f[...] = pbuf[...].reshape(768, 128).astype(F32)
    for s in range(4):
        pltpu.make_async_copy(hbuf.at[0, s], hbuf.at[0, s], r_sib.at[s]).wait()
    projected = jnp.zeros((24, 128), F32)
    for k in range(2):
        for s in range(4):
            parts = []
            for f in range(4):
                r = (s * 4 + f) * 2 if k == 0 else (f * 4 + s) * 2 + 1
                parts.append(pool_f[pl.ds(r, 24, stride=32), :])
            lhs = jnp.concatenate(parts, axis=1).astype(BF16)
            projected += jnp.dot(lhs, hbuf[k, s].reshape(512, 128), preferred_element_type=F32)
    resid = projected.astype(BF16).astype(F32) - cents
    resid = jnp.concatenate([resid, jnp.zeros((8, 128), F32)], axis=0).astype(BF16)

    loads[6].wait()
    partial = jnp.dot(resid, rot_v[...], preferred_element_type=F32)
    for j in range(8):
        part_send[j] = partial[:, j * 128 : (j + 1) * 128].astype(BF16)
    for d in range(1, 8):
        to = lax.rem(m + d, 8)
        pltpu.make_async_remote_copy(
            part_send.at[to], part_recv.at[m], s_part, r_part, device_id=(g, to), device_id_type=MESH
        ).start()
    part_recv[m] = part_send[m]
    wait_many(part_recv.at[pl.ds(0, 7)], r_part)
    rotated = jnp.sum(part_recv[...].astype(F32), axis=0)[:24]
    size = jnp.abs(rotated)
    left = iota((24, 128), 1) < 64
    s0 = jnp.max(jnp.where(left, size, 0.0), axis=1, keepdims=True) + 1e-06
    s1 = jnp.max(jnp.where(left, 0.0, size), axis=1, keepdims=True) + 1e-06
    codes_ref[...] = (rotated / jnp.where(left, s0, s1)).astype(BF16)
    scales_ref[...] = jnp.where(iota((24, 2), 1) == 0, s0, s1).astype(BF16)

    wait_many(hbuf.at[0, 0, pl.ds(0, 3)], s_h1)
    wait_many(hbuf.at[0, pl.ds(0, 3)], s_h2)
    wait_many(hbuf.at[0], s_sib)
    wait_many(ids_all.at[pl.ds(0, 31)], s_ids)
    wait_many(row_send.at[pl.ds(0, 31)], s_row)
    for p in range(3):
        wait_many(pbuf.at[pl.ds(0, 7), p], s_pool.at[p])
    wait_many(part_send.at[pl.ds(0, 7)], s_part)


def per_device(hidden, lengths, list_ids, gain, head, list_slot, centroids, rotation):
    dma = pltpu.SemaphoreType.DMA
    return pl.pallas_call(
        kernel,
        out_shape=(
            jax.ShapeDtypeStruct((24, 128), BF16),
            jax.ShapeDtypeStruct((24, 2), BF16),
        ),
        in_specs=[pl.BlockSpec(memory_space=pl.ANY)] * 8,
        out_specs=(
            pl.BlockSpec(memory_space=pltpu.VMEM),
            pl.BlockSpec(memory_space=pltpu.VMEM),
        ),
        scratch_shapes=[
            pltpu.VMEM((3, 256, 4096), BF16),
            pltpu.VMEM((1, 3), jnp.int32),
            pltpu.VMEM((32, 1, 24), jnp.int32),
            pltpu.VMEM((32, 128), BF16),
            pltpu.VMEM((2, 4, 4, 128, 128), BF16),
            pltpu.VMEM((16, 128), jnp.int32),
            pltpu.VMEM((2048, 128), BF16),
            pltpu.VMEM((128, 1024), BF16),
            pltpu.VMEM((32, 2, 128), F32),
            pltpu.VMEM((32, 2, 128), F32),
            pltpu.VMEM((3, 32, 128), F32),
            pltpu.VMEM((8, 3, 32, 128), BF16),
            pltpu.VMEM((768, 128), F32),
            pltpu.VMEM((8, 32, 128), BF16),
            pltpu.VMEM((8, 32, 128), BF16),
            dma((7,)), dma((6,)),
            dma, dma,
            dma, dma,
            dma((3,)), dma((3,)),
            dma, dma,
            dma, dma((4,)),
            dma, dma((4,)),
            dma, dma,
        ],
        compiler_params=pltpu.CompilerParams(
            collective_id=0, has_side_effects=True, vmem_limit_bytes=56 * 2**20
        ),
    )(
        hidden,
        lengths.reshape(1, 3),
        list_ids.reshape(1, 24),
        gain.reshape(32, 128),
        head,
        list_slot.reshape(32, 16, 128),
        centroids,
        rotation,
    )


def solution(mesh):
    in_specs = (
        P(("dp", "mp"), None, None),
        P(("dp", "mp")),
        P("dp"),
        P(),
        P("dp", "mp"),
        P(),
        P("dp", None),
        P("mp", None),
    )
    out_specs = (P("dp", "mp"), P("dp", "mp"))
    return jax.shard_map(
        per_device, mesh=mesh, in_specs=in_specs, out_specs=out_specs, check_vma=False
    )
```

```python
import jax
import jax.numpy as jnp
from jax import lax
from jax.experimental import pallas as pl
from jax.experimental.pallas import tpu as pltpu
from jax.sharding import PartitionSpec as P

MESH = pl.DeviceIdType.MESH
F32 = jnp.float32
BF16 = jnp.bfloat16
EPS = 1e-05
HALF = 128
NT = (((1,), (1,)), ((), ()))
Z_ORDER = (4, 3, 5, 2, 6, 1, 7)
AROUND = (2, 1, 3, 0)
PLANE = [(i, j) for i in AROUND for j in AROUND][:-1]
PLANE.sort(key=lambda o: -min(o[0], 4 - o[0]) - min(o[1], 4 - o[1]))


def iota(shape, axis):
    return lax.broadcasted_iota(jnp.int32, shape, axis)


def kernel(
    hidden, lengths, list_ids, gain, head, list_slot, centroids, rotation,
    rot_ref,
    hid_v, len_v, ids_all, gain_v, hbuf, slot_v, cent_v, rot_v,
    row_f, row_send, row_recv, rcol, pool_t, gain_t, psend, pbuf, pool_f, part_send, part_recv,
    sem_loc, sem_hid, s_ids, r_ids, s_row, r_row, s_pool, r_pool,
    s_head, r_head, s_part, r_part, s_rot, r_rot, s_sib, r_sib,
):
    g = lax.axis_index("dp")
    m = lax.axis_index("mp")
    core = lax.rem(g, 2)
    chip = g // 2
    x = lax.rem(chip, 4)
    y = chip // 4

    def away(dx, dy, k):
        return 2 * (4 * lax.rem(y + dy, 4) + lax.rem(x + dx, 4)) + k

    def local(src, dst, i):
        return pltpu.make_async_copy(src, dst, sem_loc.at[i])

    def remote(src, dst, send, recv, dp, mp):
        return pltpu.make_async_remote_copy(
            src, dst, send, recv, device_id=(dp, mp), device_id_type=MESH
        )

    def wait_many(ref, sem):
        pltpu.make_async_copy(ref, ref, sem).wait()

    loads = [
        local(head, hbuf.at[chip], 0),
        local(list_ids, ids_all.at[g], 1),
        local(lengths, len_v, 2),
        local(gain, gain_v, 3),
        local(list_slot.at[g], slot_v, 4),
        local(centroids, cent_v, 5),
        local(rotation, rot_v, 6),
    ]
    chunks = []
    for p in range(3):
        for h in range(2):
            rows = pl.ds(h * HALF, HALF)
            chunks.append(
                pltpu.make_async_copy(
                    hidden.at[p, rows], hid_v.at[p, rows], sem_hid.at[2 * p + h]
                )
            )
    for c in loads[:4]:
        c.start()
    for c in chunks:
        c.start()
    for c in loads[4:]:
        c.start()

    barrier = pltpu.get_barrier_semaphore()

    def greet_plane(i, carry):
        pl.semaphore_signal(
            barrier, inc=1, device_id=(lax.rem(g + 1 + i, 32), m), device_id_type=MESH
        )
        return carry

    def greet_z(i, carry):
        to = lax.rem(m + 1 + i, 8)
        for k in range(2):
            pl.semaphore_signal(
                barrier, inc=1, device_id=(2 * chip + k, to), device_id_type=MESH
            )
        return carry

    lax.fori_loop(0, 31, greet_plane, 0)
    lax.fori_loop(0, 7, greet_z, 0)

    loads[2].wait()
    loads[3].wait()
    gain_t[...] = gain_v[...].astype(F32)
    ones = jnp.ones((8, 128), BF16)

    def pool(p):
        total = jnp.zeros((8, 4096), F32)
        length = len_v[:, p : p + 1]
        for h in range(2):
            chunks[2 * p + h].wait()
            rows = pl.ds(h * HALF, HALF)
            acc = jnp.zeros((HALF, 128), F32)
            for c in range(32):
                v = hid_v[p, rows, c * 128 : (c + 1) * 128].astype(F32)
                acc += v * v
            hi = acc.astype(BF16)
            lo = (acc - hi.astype(F32)).astype(BF16)
            square = lax.dot_general(ones, hi, NT, preferred_element_type=F32)
            square += lax.dot_general(ones, lo, NT, preferred_element_type=F32)
            token = iota((8, HALF), 1) + h * HALF
            w = jnp.where(token < length, lax.rsqrt(square * (1.0 / 4096) + EPS), 0.0)
            w = w / length.astype(F32)
            w_hi = w.astype(BF16).astype(F32)
            which = iota((8, HALF), 0)
            lhs = jnp.where(which == 0, w_hi, jnp.where(which == 1, w - w_hi, 0.0)).astype(BF16)
            total += jnp.dot(lhs, hid_v[p, rows, :], preferred_element_type=F32)
        line = total[0:1] + total[1:2]
        for c in range(32):
            pool_t[p, c : c + 1, :] = line[:, c * 128 : (c + 1) * 128]
        for k in range(2):
            half = pl.ds(k, 16, stride=2)
            psend[k, p] = (pool_t[p, half, :] * gain_t[half, :]).astype(BF16)

    def send_pooled(first, count, i):
        rows = pl.ds(first, count)
        dst = pbuf.at[core * 8 + m, rows]
        for d in Z_ORDER:
            to = lax.rem(m + d, 8)
            for k in range(2):
                remote(psend.at[k, rows], dst, s_pool.at[i], r_pool.at[i], 2 * chip + k, to).start()
        remote(
            psend.at[1 - core, rows], dst, s_pool.at[i], r_pool.at[i], 2 * chip + 1 - core, m
        ).start()

    pool(0)
    pool(1)
    loads[0].wait()
    loads[1].wait()
    pl.semaphore_wait(barrier, 45)

    mine = ids_all.at[g]
    block = hbuf.at[chip]
    for dx, dy in PLANE:
        for k in range(2):
            remote(mine, mine, s_ids, r_ids, away(dx, dy, k), m).start()
    remote(mine, mine, s_ids, r_ids, 2 * chip + 1 - core, m).start()
    for dx, dy in PLANE:
        remote(block, block, s_head, r_head, away(dx, dy, core), m).start()
    send_pooled(0, 2, 0)
    pool(2)
    send_pooled(2, 1, 1)
    pbuf[core * 8 + m] = psend[core]

    loads[6].wait()
    half = pl.ds(pl.multiple_of(core * 64, 64), 64)

    def columns(j):
        return rot_v.at[half, pl.ds(pl.multiple_of(j * 128, 128), 128)]

    for d in Z_ORDER:
        to = lax.rem(m + d, 8)
        remote(columns(to), rcol.at[core, m], s_rot, r_rot, g, to).start()
    keep = local(columns(m), rcol.at[core, m], 7)
    keep.start()

    loads[4].wait()
    loads[5].wait()
    wait_many(ids_all.at[pl.ds(0, 31)], r_ids)
    ids = ids_all[:, 0, :]
    match = (ids >> 11) == g
    key = (iota(ids.shape, 1) * 2048 + (ids & 2047)).astype(F32)
    k0 = jnp.min(jnp.where(match, key, 1e6), axis=1, keepdims=True)
    k1 = jnp.max(jnp.where(match, key, -1.0), axis=1, keepdims=True)
    wanted = jnp.concatenate([k0, k1], axis=0).astype(jnp.int32) & 2047
    column = iota((64, 128), 1)
    found = jnp.zeros((64, 128), F32)
    for c in range(16):
        slots = (slot_v[c : c + 1, :] & 2047).astype(F32)
        found += jnp.where(wanted == column + c * 128, slots, 0.0)
    found = jnp.sum(found, axis=1, keepdims=True)
    column = column.astype(F32)
    hot = [
        jnp.where(found == column + c * 128.0, 1.0, 0.0).astype(BF16) for c in range(16)
    ]
    picked = jnp.dot(jnp.concatenate(hot, axis=1), cent_v[...], preferred_element_type=F32)
    for r in range(2):
        for c in range(8):
            row_f[pl.ds(8 * r + c, 32, stride=16), :] = picked[
                32 * r : 32 * r + 32, c * 128 : (c + 1) * 128
            ]
    row_send[...] = row_f[...].astype(BF16).reshape(32, 16, 128)
    for dx, dy in PLANE:
        for k in range(2):
            to = away(dx, dy, k)
            remote(row_send.at[to], row_recv.at[g], s_row, r_row, to, m).start()
    to = 2 * chip + 1 - core
    remote(row_send.at[to], row_recv.at[g], s_row, r_row, to, m).start()
    row_recv[g] = row_send[g]

    keep.wait()
    wait_many(rcol.at[0, pl.ds(0, 7)], r_rot)
    remote(rcol.at[core], rcol.at[core], s_sib, r_sib, 2 * chip + 1 - core, m).start()

    mine = (ids_all[g] >> 11).astype(F32)
    r24 = iota((24, 24), 0)
    c24 = iota((24, 24), 1)
    along = jnp.broadcast_to(mine, (24, 24))
    owner = jnp.sum(jnp.where(r24 == c24, along, 0.0), axis=1, keepdims=True)
    again = jnp.max(jnp.where((along == owner) & (c24 < r24), 1.0, 0.0), axis=1, keepdims=True)
    here = jnp.where(owner == iota((24, 32), 1).astype(F32), 1.0, 0.0)
    take = jnp.concatenate([here * (1.0 - again), here * again], axis=1).astype(BF16)

    wait_many(pbuf.at[pl.ds(0, 15), pl.ds(0, 2)], r_pool.at[0])
    wait_many(pbuf.at[pl.ds(0, 15), pl.ds(2, 1)], r_pool.at[1])
    pool_f[...] = pbuf[...].reshape(768, 128).astype(F32)
    lhs = jnp.concatenate([pool_f[pl.ds(c, 48, stride=16), :] for c in range(16)], axis=1)
    lhs = lhs.astype(BF16)
    wait_many(hbuf.at[pl.ds(0, 15)], r_head)
    projected = jnp.dot(lhs, hbuf[...].reshape(2048, 128), preferred_element_type=F32)

    pad = jnp.zeros((8, 128), F32)
    projected = jnp.concatenate([projected[:24], pad, projected[24:], pad], axis=0).astype(BF16)

    partial = jnp.dot(projected, rot_v[...], preferred_element_type=F32)
    for q in range(2):
        for j in range(8):
            part_send[q, j] = partial[32 * q : 32 * q + 32, j * 128 : (j + 1) * 128].astype(BF16)
    dst = part_recv.at[core * 8 + m]
    for d in Z_ORDER:
        to = lax.rem(m + d, 8)
        for q in range(2):
            remote(part_send.at[q, to], dst, s_part, r_part, 2 * chip + q, to).start()
    remote(part_send.at[1 - core, m], dst, s_part, r_part, 2 * chip + 1 - core, m).start()
    part_recv[core * 8 + m] = part_send[core, m]

    wait_many(row_recv.at[pl.ds(0, 31)], r_row)
    row_f[...] = row_recv[...].reshape(512, 128).astype(F32)
    rows = [
        jnp.concatenate(
            [row_f[pl.ds(8 * r + c, 32, stride=16), :] for c in range(8)], axis=1
        )
        for r in range(2)
    ]
    rows = jnp.concatenate(rows, axis=0).astype(BF16)
    cents = jnp.dot(take, rows, preferred_element_type=F32).astype(BF16)
    wait_many(rcol.at[1 - core], r_sib)
    turn = jnp.concatenate([rcol[k, j] for j in range(8) for k in range(2)], axis=0)
    turned = jnp.dot(cents, turn, preferred_element_type=F32)

    wait_many(part_recv.at[pl.ds(0, 15)], r_part)
    rot_ref[...] = jnp.sum(part_recv[...].astype(F32), axis=0)[:24] - turned

    wait_many(hbuf.at[pl.ds(0, 15)], s_head)
    wait_many(ids_all.at[pl.ds(0, 31)], s_ids)
    wait_many(row_send.at[pl.ds(0, 31)], s_row)
    wait_many(pbuf.at[pl.ds(0, 15), pl.ds(0, 2)], s_pool.at[0])
    wait_many(pbuf.at[pl.ds(0, 15), pl.ds(2, 1)], s_pool.at[1])
    wait_many(part_recv.at[pl.ds(0, 15)], s_part)
    wait_many(rcol.at[0, pl.ds(0, 7)], s_rot)
    wait_many(rcol.at[0], s_sib)


def quantize(rot_ref, codes_ref, scales_ref):
    rotated = rot_ref[...]
    size = jnp.abs(rotated)
    left = iota((24, 128), 1) < 64
    s0 = jnp.max(jnp.where(left, size, 0.0), axis=1, keepdims=True) + 1e-06
    s1 = jnp.max(jnp.where(left, 0.0, size), axis=1, keepdims=True) + 1e-06
    codes_ref[...] = (rotated / jnp.where(left, s0, s1)).astype(BF16)
    r24 = iota((24, 24), 0)
    c24 = iota((24, 24), 1)
    s0 = jnp.sum(jnp.where(r24 == c24, s0, 0.0), axis=0, keepdims=True)
    s1 = jnp.sum(jnp.where(r24 == c24, s1, 0.0), axis=0, keepdims=True)
    scales_ref[...] = jnp.concatenate([s0, s1], axis=0).astype(BF16)


def per_device(hidden, lengths, list_ids, gain, head, list_slot, centroids, rotation):
    dma = pltpu.SemaphoreType.DMA
    rotated = pl.pallas_call(
        kernel,
        out_shape=jax.ShapeDtypeStruct((24, 128), F32),
        in_specs=[pl.BlockSpec(memory_space=pl.ANY)] * 8,
        out_specs=pl.BlockSpec(memory_space=pltpu.VMEM),
        scratch_shapes=[
            pltpu.VMEM((3, 256, 4096), BF16),
            pltpu.VMEM((1, 3), jnp.int32),
            pltpu.VMEM((32, 1, 24), jnp.int32),
            pltpu.VMEM((32, 128), BF16),
            pltpu.VMEM((16, 128, 128), BF16),
            pltpu.VMEM((16, 128), jnp.int32),
            pltpu.VMEM((2048, 1024), BF16),
            pltpu.VMEM((128, 1024), BF16),
            pltpu.VMEM((512, 128), F32),
            pltpu.VMEM((32, 16, 128), BF16),
            pltpu.VMEM((32, 16, 128), BF16),
            pltpu.VMEM((2, 8, 64, 128), BF16),
            pltpu.VMEM((3, 32, 128), F32),
            pltpu.VMEM((32, 128), F32),
            pltpu.VMEM((2, 3, 16, 128), BF16),
            pltpu.VMEM((16, 3, 16, 128), BF16),
            pltpu.VMEM((768, 128), F32),
            pltpu.VMEM((2, 8, 32, 128), BF16),
            pltpu.VMEM((16, 32, 128), BF16),
            dma((8,)), dma((6,)),
            dma, dma,
            dma, dma,
            dma((2,)), dma((2,)),
            dma, dma,
            dma, dma,
            dma, dma,
            dma, dma,
        ],
        compiler_params=pltpu.CompilerParams(
            collective_id=0, has_side_effects=True, vmem_limit_bytes=56 * 2**20
        ),
    )(
        hidden,
        lengths.reshape(1, 3),
        list_ids.reshape(1, 24),
        gain.reshape(32, 128),
        head,
        list_slot.reshape(32, 16, 128),
        centroids,
        rotation,
    )
    codes, scales = pl.pallas_call(
        quantize,
        out_shape=(
            jax.ShapeDtypeStruct((24, 128), BF16),
            jax.ShapeDtypeStruct((2, 24), BF16),
        ),
        in_specs=[pl.BlockSpec(memory_space=pltpu.VMEM)],
        out_specs=(
            pl.BlockSpec(memory_space=pltpu.VMEM),
            pl.BlockSpec(memory_space=pltpu.VMEM),
        ),
    )(rotated)
    return codes, scales.T


def solution(mesh):
    in_specs = (
        P(("dp", "mp"), None, None),
        P(("dp", "mp")),
        P("dp"),
        P(),
        P("dp", "mp"),
        P(),
        P("dp", None),
        P("mp", None),
    )
    out_specs = (P("dp", "mp"), P("dp", "mp"))
    return jax.shard_map(
        per_device, mesh=mesh, in_specs=in_specs, out_specs=out_specs, check_vma=False
    )
```

```python
import jax
import jax.numpy as jnp
from jax import lax
from jax.experimental import pallas as pl
from jax.experimental.pallas import tpu as pltpu
from jax.sharding import PartitionSpec as P

MESH = pl.DeviceIdType.MESH
F32 = jnp.float32
BF16 = jnp.bfloat16
EPS = 1e-05
HALF = 128
NT = (((1,), (1,)), ((), ()))
Z_ORDER = (4, 3, 5, 2, 6, 1, 7)
AROUND = (2, 1, 3, 0)
PLANE = [(i, j) for i in AROUND for j in AROUND][:-1]


def hops(dx, dy):
    return min(dx, 4 - dx) + min(dy, 4 - dy)


PLANE.sort(key=lambda o: -hops(*o))


def iota(shape, axis):
    return lax.broadcasted_iota(jnp.int32, shape, axis)


def kernel(
    hidden, lengths, list_ids, gain, head, list_slot, centroids, rotation,
    rot_ref,
    hid_v, len_v, ids_v, ids_all, gain_v, hbuf, slot_v, cent_v, rot_v,
    row_f, row_send, row_recv, rcol, pool_t, gain_t, psend, pbuf, pool_f, part_send, part_recv,
    sem_loc, sem_hid, s_ids, r_ids, s_row, r_row, s_pool, r_pool,
    s_head, r_head, s_part, r_part, s_rot, r_rot, s_sib, r_sib,
):
    g = lax.axis_index("dp")
    m = lax.axis_index("mp")
    core = lax.rem(g, 2)
    chip = g // 2
    x = lax.rem(chip, 4)
    y = chip // 4

    def away(dx, dy, k):
        return 2 * (4 * lax.rem(y + dy, 4) + lax.rem(x + dx, 4)) + k

    def local(src, dst, i):
        return pltpu.make_async_copy(src, dst, sem_loc.at[i])

    def remote(src, dst, send, recv, dp, mp):
        return pltpu.make_async_remote_copy(
            src, dst, send, recv, device_id=(dp, mp), device_id_type=MESH
        )

    def wait_many(ref, sem):
        pltpu.make_async_copy(ref, ref, sem).wait()

    loads = [
        local(head, hbuf.at[chip], 0),
        local(list_ids, ids_v, 1),
        local(lengths, len_v, 2),
        local(gain, gain_v, 3),
        local(list_slot, slot_v, 4),
        local(centroids, cent_v, 5),
        local(rotation, rot_v, 6),
    ]
    chunks = []
    for p in range(3):
        for h in range(2):
            rows = pl.ds(h * HALF, HALF)
            chunks.append(
                pltpu.make_async_copy(
                    hidden.at[p, rows], hid_v.at[p, rows], sem_hid.at[2 * p + h]
                )
            )
    for c in loads[:4]:
        c.start()
    for c in chunks[:2]:
        c.start()
    barrier = pltpu.get_barrier_semaphore()

    def greet(dp, mp):
        pl.semaphore_signal(barrier, inc=1, device_id=(dp, mp), device_id_type=MESH)

    for far in (4, 3, 2, 1):
        for d in (far, 8 - far)[: 1 if far == 4 else 2]:
            for k in range(2):
                greet(2 * chip + k, lax.rem(m + d, 8))
        for dx, dy in PLANE:
            if hops(dx, dy) == far:
                for k in range(2):
                    greet(away(dx, dy, k), m)
    greet(2 * chip + 1 - core, m)

    loads[4].start()
    for c in chunks[2:]:
        c.start()
    for c in loads[5:]:
        c.start()

    loads[2].wait()
    loads[3].wait()
    gain_t[...] = gain_v[...].astype(F32)
    ones = jnp.ones((8, 128), BF16)

    def weigh(i):
        p, h = i // 2, i % 2
        chunks[i].wait()
        rows = pl.ds(h * HALF, HALF)
        length = len_v[:, p : p + 1]
        acc = jnp.zeros((HALF, 128), F32)
        for c in range(32):
            v = hid_v[p, rows, c * 128 : (c + 1) * 128].astype(F32)
            acc += v * v
        hi = acc.astype(BF16)
        lo = (acc - hi.astype(F32)).astype(BF16)
        square = lax.dot_general(ones, hi, NT, preferred_element_type=F32)
        square += lax.dot_general(ones, lo, NT, preferred_element_type=F32)
        token = iota((8, HALF), 1) + h * HALF
        w = jnp.where(token < length, lax.rsqrt(square * (1.0 / 4096) + EPS), 0.0)
        w = w / length.astype(F32)
        w_hi = w.astype(BF16).astype(F32)
        which = iota((8, HALF), 0)
        return jnp.where(which == 0, w_hi, jnp.where(which == 1, w - w_hi, 0.0)).astype(BF16)

    def add_up(i, lhs, total):
        p, h = i // 2, i % 2
        part = jnp.dot(lhs, hid_v[p, pl.ds(h * HALF, HALF), :], preferred_element_type=F32)
        if h == 0:
            return part
        total = total + part
        line = total[0:1] + total[1:2]
        for c in range(32):
            pool_t[p, c : c + 1, :] = line[:, c * 128 : (c + 1) * 128]
        for k in range(2):
            half = pl.ds(k, 16, stride=2)
            psend[k, p] = (pool_t[p, half, :] * gain_t[half, :]).astype(BF16)
        return None

    def pool(first, last, lhs, total):
        for i in range(first, last):
            now = weigh(i) if i < 6 else None
            if i > 0:
                total = add_up(i - 1, lhs, total)
            lhs = now
        return lhs, total


    lhs, total = pool(0, 4, None, None)

    loads[1].wait()
    loads[4].wait()
    r24 = iota((24, 24), 0)
    c24 = iota((24, 24), 1)

    def turn(v, axis):
        return jnp.sum(jnp.where(r24 == c24, v, 0.0), axis=axis, keepdims=True)

    along = jnp.broadcast_to(ids_v[...].astype(F32), (24, 24))
    ids = turn(along, 1).astype(jnp.int32)
    table = slot_v[...]
    hot = jnp.where(iota((24, 512), 1) == (ids >> 7), 1.0, 0.0).astype(BF16)
    found = 256.0 * jnp.dot(hot, (table >> 8).astype(F32).astype(BF16), preferred_element_type=F32)
    found += jnp.dot(hot, (table & 255).astype(F32).astype(BF16), preferred_element_type=F32)
    found = jnp.where(iota((24, 128), 1) == (ids & 127), found, 0.0)
    slots = jnp.sum(found, axis=1, keepdims=True)
    ids_all[g] = turn(slots, 0).astype(jnp.int32)
    owner = (slots.astype(jnp.int32) >> 11).astype(F32)
    along = jnp.broadcast_to(turn(owner, 0), (24, 24))
    again = jnp.max(jnp.where((along == owner) & (c24 < r24), 1.0, 0.0), axis=1, keepdims=True)
    here = jnp.where(owner == iota((24, 32), 1).astype(F32), 1.0, 0.0)
    take = jnp.concatenate([here * (1.0 - again), here * again], axis=1).astype(BF16)

    loads[0].wait()
    pl.semaphore_wait(barrier, 45)

    mine = ids_all.at[g]
    block = hbuf.at[chip]
    pooled = pbuf.at[core * 8 + m]
    for dx, dy in PLANE:
        for k in range(2):
            remote(mine, mine, s_ids, r_ids, away(dx, dy, k), m).start()
    remote(mine, mine, s_ids, r_ids, 2 * chip + 1 - core, m).start()
    for dx, dy in PLANE:
        remote(block, block, s_head, r_head, away(dx, dy, core), m).start()
    pool(4, 7, lhs, total)
    for d in Z_ORDER:
        to = lax.rem(m + d, 8)
        for k in range(2):
            remote(psend.at[k], pooled, s_pool, r_pool, 2 * chip + k, to).start()
    remote(psend.at[1 - core], pooled, s_pool, r_pool, 2 * chip + 1 - core, m).start()
    pbuf[core * 8 + m] = psend[core]

    loads[6].wait()
    half = pl.ds(pl.multiple_of(core * 64, 64), 64)

    def columns(j):
        return rot_v.at[half, pl.ds(pl.multiple_of(j * 128, 128), 128)]

    for d in Z_ORDER:
        to = lax.rem(m + d, 8)
        remote(columns(to), rcol.at[core, m], s_rot, r_rot, g, to).start()
    keep = local(columns(m), rcol.at[core, m], 7)
    keep.start()

    loads[5].wait()
    wait_many(ids_all.at[pl.ds(0, 31)], r_ids)
    ids = ids_all[:, 0, :]
    match = (ids >> 11) == g
    key = (iota(ids.shape, 1) * 2048 + (ids & 2047)).astype(F32)
    k0 = jnp.min(jnp.where(match, key, 1e6), axis=1, keepdims=True)
    k1 = jnp.max(jnp.where(match, key, -1.0), axis=1, keepdims=True)
    wanted = jnp.concatenate([k0, k1], axis=0).astype(jnp.int32) & 2047
    column = iota((64, 128), 1)
    hot = [jnp.where(wanted == column + c * 128, 1.0, 0.0).astype(BF16) for c in range(16)]
    picked = jnp.dot(jnp.concatenate(hot, axis=1), cent_v[...], preferred_element_type=F32)
    for r in range(2):
        for c in range(8):
            row_f[pl.ds(8 * r + c, 32, stride=16), :] = picked[
                32 * r : 32 * r + 32, c * 128 : (c + 1) * 128
            ]
    row_send[...] = row_f[...].astype(BF16).reshape(32, 16, 128)
    for dx, dy in PLANE:
        for k in range(2):
            to = away(dx, dy, k)
            remote(row_send.at[to], row_recv.at[g], s_row, r_row, to, m).start()
    to = 2 * chip + 1 - core
    remote(row_send.at[to], row_recv.at[g], s_row, r_row, to, m).start()
    row_recv[g] = row_send[g]

    wait_many(pbuf.at[pl.ds(0, 15)], r_pool)
    pool_f[...] = pbuf[...].reshape(768, 128).astype(F32)
    lhs = jnp.concatenate([pool_f[pl.ds(c, 48, stride=16), :] for c in range(16)], axis=1)
    lhs = lhs.astype(BF16)
    wait_many(hbuf.at[pl.ds(0, 15)], r_head)
    projected = jnp.dot(lhs, hbuf[...].reshape(2048, 128), preferred_element_type=F32)

    pad = jnp.zeros((8, 128), F32)
    projected = jnp.concatenate([projected[:24], pad, projected[24:], pad], axis=0).astype(BF16)

    partial = jnp.dot(projected, rot_v[...], preferred_element_type=F32)
    for q in range(2):
        for j in range(8):
            part_send[q, j] = partial[32 * q : 32 * q + 32, j * 128 : (j + 1) * 128].astype(BF16)
    dst = part_recv.at[core * 8 + m]
    for d in Z_ORDER:
        to = lax.rem(m + d, 8)
        for q in range(2):
            remote(part_send.at[q, to], dst, s_part, r_part, 2 * chip + q, to).start()
    remote(part_send.at[1 - core, m], dst, s_part, r_part, 2 * chip + 1 - core, m).start()
    part_recv[core * 8 + m] = part_send[core, m]

    keep.wait()
    wait_many(rcol.at[0, pl.ds(0, 7)], r_rot)
    remote(rcol.at[core], rcol.at[core], s_sib, r_sib, 2 * chip + 1 - core, m).start()

    wait_many(row_recv.at[pl.ds(0, 31)], r_row)
    row_f[...] = row_recv[...].reshape(512, 128).astype(F32)
    rows = [
        jnp.concatenate(
            [row_f[pl.ds(8 * r + c, 32, stride=16), :] for c in range(8)], axis=1
        )
        for r in range(2)
    ]
    rows = jnp.concatenate(rows, axis=0).astype(BF16)
    cents = jnp.dot(take, rows, preferred_element_type=F32).astype(BF16)
    wait_many(rcol.at[1 - core], r_sib)
    wheel = jnp.concatenate([rcol[k, j] for j in range(8) for k in range(2)], axis=0)
    turned = jnp.dot(cents, wheel, preferred_element_type=F32)

    wait_many(part_recv.at[pl.ds(0, 15)], r_part)
    rot_ref[...] = jnp.sum(part_recv[...].astype(F32), axis=0)[:24] - turned

    wait_many(hbuf.at[pl.ds(0, 15)], s_head)
    wait_many(ids_all.at[pl.ds(0, 31)], s_ids)
    wait_many(row_send.at[pl.ds(0, 31)], s_row)
    wait_many(pbuf.at[pl.ds(0, 15)], s_pool)
    wait_many(part_recv.at[pl.ds(0, 15)], s_part)
    wait_many(rcol.at[0, pl.ds(0, 7)], s_rot)
    wait_many(rcol.at[0], s_sib)


def quantize(rot_ref, codes_ref, scales_ref):
    rotated = rot_ref[...]
    size = jnp.abs(rotated)
    left = iota((24, 128), 1) < 64
    s0 = jnp.max(jnp.where(left, size, 0.0), axis=1, keepdims=True) + 1e-06
    s1 = jnp.max(jnp.where(left, 0.0, size), axis=1, keepdims=True) + 1e-06
    codes_ref[...] = (rotated / jnp.where(left, s0, s1)).astype(BF16)
    r24 = iota((24, 24), 0)
    c24 = iota((24, 24), 1)
    s0 = jnp.sum(jnp.where(r24 == c24, s0, 0.0), axis=0, keepdims=True)
    s1 = jnp.sum(jnp.where(r24 == c24, s1, 0.0), axis=0, keepdims=True)
    scales_ref[...] = jnp.concatenate([s0, s1], axis=0).astype(BF16)


def per_device(hidden, lengths, list_ids, gain, head, list_slot, centroids, rotation):
    dma = pltpu.SemaphoreType.DMA
    rotated = pl.pallas_call(
        kernel,
        out_shape=jax.ShapeDtypeStruct((24, 128), F32),
        in_specs=[pl.BlockSpec(memory_space=pl.ANY)] * 8,
        out_specs=pl.BlockSpec(memory_space=pltpu.VMEM),
        scratch_shapes=[
            pltpu.VMEM((3, 256, 4096), BF16),
            pltpu.VMEM((1, 3), jnp.int32),
            pltpu.VMEM((1, 24), jnp.int32),
            pltpu.VMEM((32, 1, 24), jnp.int32),
            pltpu.VMEM((32, 128), BF16),
            pltpu.VMEM((16, 128, 128), BF16),
            pltpu.VMEM((512, 128), jnp.int32),
            pltpu.VMEM((2048, 1024), BF16),
            pltpu.VMEM((128, 1024), BF16),
            pltpu.VMEM((512, 128), F32),
            pltpu.VMEM((32, 16, 128), BF16),
            pltpu.VMEM((32, 16, 128), BF16),
            pltpu.VMEM((2, 8, 64, 128), BF16),
            pltpu.VMEM((3, 32, 128), F32),
            pltpu.VMEM((32, 128), F32),
            pltpu.VMEM((2, 3, 16, 128), BF16),
            pltpu.VMEM((16, 3, 16, 128), BF16),
            pltpu.VMEM((768, 128), F32),
            pltpu.VMEM((2, 8, 32, 128), BF16),
            pltpu.VMEM((16, 32, 128), BF16),
            dma((8,)), dma((6,)),
            dma, dma,
            dma, dma,
            dma, dma,
            dma, dma,
            dma, dma,
            dma, dma,
            dma, dma,
        ],
        compiler_params=pltpu.CompilerParams(
            collective_id=0, has_side_effects=True, vmem_limit_bytes=56 * 2**20
        ),
    )(
        hidden,
        lengths.reshape(1, 3),
        list_ids.reshape(1, 24),
        gain.reshape(32, 128),
        head,
        list_slot.reshape(512, 128),
        centroids,
        rotation,
    )
    codes, scales = pl.pallas_call(
        quantize,
        out_shape=(
            jax.ShapeDtypeStruct((24, 128), BF16),
            jax.ShapeDtypeStruct((2, 24), BF16),
        ),
        in_specs=[pl.BlockSpec(memory_space=pltpu.VMEM)],
        out_specs=(
            pl.BlockSpec(memory_space=pltpu.VMEM),
            pl.BlockSpec(memory_space=pltpu.VMEM),
        ),
    )(rotated)
    return codes, scales.T


def solution(mesh):
    in_specs = (
        P(("dp", "mp"), None, None),
        P(("dp", "mp")),
        P("dp"),
        P(),
        P("dp", "mp"),
        P(),
        P("dp", None),
        P("mp", None),
    )
    out_specs = (P("dp", "mp"), P("dp", "mp"))
    return jax.shard_map(
        per_device, mesh=mesh, in_specs=in_specs, out_specs=out_specs, check_vma=False
    )
```
